32 devices in a mesh: videos: 2 (over y), rows: 4 (over z), cols: 4 (over x, core).
Axes of the slice: x: 2, y: 2, z: 4, core: 2. Of those that a mesh axis runs over, the one named last changes fastest.
Arguments:
- hidden: bfloat16 [2, 16, 128, 384], P('videos', 'rows', 'cols'), parts along dimension 0, may hold values from -40 to 40
- frame_cache: bfloat16 [2, 2, 16, 128, 384], P('videos', None, 'rows', 'cols'), parts along dimension 0, may hold values from -6 to 6
- shortcut: bfloat16 [2, 16, 128, 384], P('videos', 'rows', 'cols'), parts along dimension 0, may hold values from -40 to 40
- gain_one: float32 [384], replicated, may hold values from 0.5 to 1.5
- conv_weight: bfloat16 [3, 3, 3, 384, 384], replicated, may hold values from -0.0625 to 0.0625
- conv_bias: float32 [384], replicated, may hold values from -2 to 2
- gain_two: float32 [384], replicated, may hold values from 0.5 to 1.5
- query_weight: bfloat16 [384, 384], replicated, may hold values from -1 to 1
- query_bias: float32 [384], replicated, may hold values from -3 to 3
- key_weight: bfloat16 [384, 384], replicated, may hold values from -1 to 1
- value_weight: bfloat16 [384, 384], replicated, may hold values from -0.3125 to 0.3125
- value_bias: float32 [384], replicated, may hold values from -3 to 3
- out_weight: bfloat16 [384, 384], replicated, may hold values from -0.3125 to 0.3125
- out_bias: float32 [384], replicated, may hold values from -2 to 2
Outputs:
- decoded: bfloat16 [2, 16, 128, 384], P('videos', 'rows', 'cols'), parts along dimension 0
The draws below stay inside these ranges and needn't reach their ends.
There are 2 independent parts, one for each index of `videos`. The reference program is written for one: setup_inputs(seed, part) draws one part's arguments, and reference() takes and returns one part's arrays. A program takes and returns all parts, laid end to end along the dimension named above; an argument that names none is the same for every part. Nothing has to cross between parts.
All inputs are finite; a program needn't handle non-finite values.
Results may differ from the reference program's by a relative error of at most 0.0065.
Values may be sent and summed in bfloat16 or wider, within the bound.
A program may use at most 128 MiB of HBM per device.

```python
import math
import jax
import jax.numpy as jnp
from jax import lax

C = 384
H = 16
W = 128


def rough_field(key):
    standard = jax.random.truncated_normal(jax.random.fold_in(key, 1), -6.0, 6.0, (1, H, W, C), jnp.float32)
    row_place = jnp.arange(H, dtype=jnp.float32) / (H - 1)
    col_place = jnp.arange(W, dtype=jnp.float32) / (W - 1)
    spread_map = (3.0 ** (row_place - 0.5))[:, None] * (3.0 ** (col_place - 0.5))[None, :]
    return (standard * spread_map[None, :, :, None]).astype(jnp.bfloat16)


def draw_hidden(key, part):
    return rough_field(jax.random.fold_in(key, 101))


def draw_shortcut(key, part):
    return rough_field(jax.random.fold_in(key, 202))


def paired_weight(key, salt):
    own_part = jax.random.truncated_normal(jax.random.fold_in(key, salt), -5.0, 5.0, (C, C), jnp.float32)
    matrix = 1.4 * own_part / math.sqrt(C)
    return jnp.clip(matrix, -1.0, 1.0).astype(jnp.bfloat16)


def draw_query_weight(key, part):
    return paired_weight(key, 401)


def draw_key_weight(key, part):
    return paired_weight(key, 402)


def block_scale(stream_key, dims, cuts, least, largest):
    def one(dim, parts):
        heights = jax.random.uniform(jax.random.fold_in(jax.random.fold_in(stream_key, 6), dim), (parts,), jnp.float32, least / len(cuts), largest / len(cuts))
        return jnp.repeat(jnp.exp(heights), dims[dim] // parts).reshape((-1,) + (1,) * (len(dims) - dim - 1))

    factor_of = one(*cuts[0])
    for cut in cuts[1:]:
        factor_of = factor_of * one(*cut)
    return factor_of


def normal_values(own_key, dims, scale, limit, cuts=(), held_as=jnp.bfloat16):
    level = block_scale(own_key, dims, cuts, -0.22, 0.18) if cuts else 1.0
    values = jax.random.normal(own_key, dims, jnp.float32) * scale * level
    return jnp.minimum(jnp.maximum(values, -limit), limit).astype(held_as)


def setup_inputs(seed: int = 0, part: int = 0) -> dict:
    keys = jax.random.split(jax.random.key(seed), 15)
    own_keys = jax.random.split(jax.random.fold_in(keys[14], part), 15)
    return {
        "hidden": draw_hidden(jax.random.fold_in(jax.random.fold_in(keys[14], part), 71), part),
        "frame_cache": normal_values(own_keys[1], (1, 2, H, W, C), 1.0, 6.0, ((2, 4), (3, 4))),
        "shortcut": draw_shortcut(jax.random.fold_in(jax.random.fold_in(keys[14], part), 71), part),
        "gain_one": jnp.clip(jax.random.uniform(keys[3], (C,), jnp.float32, 0.5, 1.5), 0.5, 1.5),
        "conv_weight": normal_values(keys[4], (3, 3, 3, C, C), (27 * C) ** -0.5, 0.0625),
        "conv_bias": normal_values(keys[5], (C,), 0.3, 2.0, (), jnp.float32),
        "gain_two": jnp.clip(jax.random.uniform(keys[6], (C,), jnp.float32, 0.5, 1.5), 0.5, 1.5),
        "query_weight": draw_query_weight(jax.random.fold_in(keys[14], 71), part),
        "query_bias": normal_values(keys[8], (C,), 0.5, 3.0, (), jnp.float32),
        "key_weight": draw_key_weight(jax.random.fold_in(keys[14], 71), part),
        "value_weight": normal_values(keys[10], (C, C), C ** -0.5, 0.3125),
        "value_bias": normal_values(keys[11], (C,), 0.5, 3.0, (), jnp.float32),
        "out_weight": normal_values(keys[12], (C, C), C ** -0.5, 0.3125),
        "out_bias": normal_values(keys[13], (C,), 0.3, 2.0, (), jnp.float32),
    }


norm_epsilon = 1e-06

def rms_norm(field, gain):
    mean_square = lax.optimization_barrier(jnp.mean(field * field, axis=-1, keepdims=True))
    return field * lax.rsqrt(mean_square + norm_epsilon) * gain

def reference(hidden, frame_cache, shortcut, gain_one, conv_weight, conv_bias, gain_two, query_weight, query_bias, key_weight, value_weight, value_bias, out_weight, out_bias):
    current = hidden[0].astype(jnp.float32)
    activated = jax.nn.silu(rms_norm(current, gain_one)).astype(jnp.bfloat16)
    stacked = jnp.concatenate([frame_cache[0], activated[None]], axis=0).astype(jnp.float32)
    convolved = lax.conv_general_dilated(stacked[None], conv_weight.astype(jnp.float32), (1, 1, 1), [(0, 0), (1, 1), (1, 1)], dimension_numbers=('NDHWC', 'DHWIO', 'NDHWC'), precision=lax.Precision.HIGHEST)[0, 0] + conv_bias
    mixed = (shortcut[0].astype(jnp.float32) + convolved).astype(jnp.bfloat16)
    normed = rms_norm(mixed.astype(jnp.float32), gain_two).astype(jnp.bfloat16)
    flat_normed = normed.reshape(H * W, C)
    queries = (jnp.dot(flat_normed, query_weight, preferred_element_type=jnp.float32) + query_bias).astype(jnp.bfloat16)
    keys_all = jnp.dot(flat_normed, key_weight, preferred_element_type=jnp.float32).astype(jnp.bfloat16)
    values = (jnp.dot(flat_normed, value_weight, preferred_element_type=jnp.float32) + value_bias).astype(jnp.bfloat16)
    score_scale = float(C) ** (-0.5)

    def attend_block(query_block):
        scores = jnp.dot(query_block, keys_all.T, preferred_element_type=jnp.float32) * score_scale
        row_max = lax.optimization_barrier(jnp.max(scores, axis=1, keepdims=True))
        expos = jnp.exp(scores - row_max)
        probabilities = expos.astype(jnp.bfloat16)
        weighted = jnp.dot(probabilities, values, preferred_element_type=jnp.float32)
        return (weighted / lax.optimization_barrier(jnp.sum(expos, axis=1, keepdims=True))).astype(jnp.bfloat16)
    attended = lax.map(attend_block, queries.reshape(H, W, C)).reshape(H * W, C)
    projected = jnp.dot(attended, out_weight, preferred_element_type=jnp.float32) + out_bias
    decoded = (mixed.reshape(H * W, C).astype(jnp.float32) + projected).astype(jnp.bfloat16)
    return decoded.reshape(1, H, W, C)
```

```python
import functools
import math

import jax
import jax.numpy as jnp
from jax import lax
from jax.experimental import pallas as pl
from jax.experimental.pallas import tpu as pltpu
from jax.sharding import PartitionSpec as P

norm_epsilon = 1e-06
f32 = jnp.float32
bf16 = jnp.bfloat16
MESH = pl.DeviceIdType.MESH


def normalize(field_rows, gain):
    mean_square = jnp.mean(field_rows * field_rows, axis=1, keepdims=True)
    return field_rows * lax.rsqrt(mean_square + norm_epsilon) * gain


def kernel(
    R, K, cores, TR, TC, C, E,
    hidden_ref, cache_ref, shortcut_ref, gain_one_ref, conv_bias_ref, gain_two_ref,
    query_bias_ref, value_bias_ref, out_bias_ref,
    conv_hbm, query_hbm, key_hbm, value_hbm, out_hbm,
    o_ref,
    conv_w, proj_w, xs, sr, sc, hr, hc, edge, G, run_max, run_sum, acc,
    conv_sem, proj_sem, hsend, hrecv, zsem, xsem, csem, rsem,
):
    X = K // cores
    N = TR * TC
    r = lax.axis_index("rows")
    col = lax.axis_index("cols")
    x = col // cores
    c = col % cores

    has_up = r > 0
    has_down = r < R - 1
    rows_ok = (has_up, None, has_down)

    def exists(dr, dc):
        ok = None
        if dr:
            ok = rows_ok[dr + 1]
        if dc:
            side = (col > 0) if dc < 0 else (col < K - 1)
            ok = side if ok is None else jnp.logical_and(ok, side)
        return ok

    neighbours = [(-1, 0), (1, 0)] + [(dr, dc) for dc in (-1, 1) for dr in (-1, 0, 1)]
    barrier = pltpu.get_barrier_semaphore()
    expected = jnp.int32(X - 1)
    for dr, dc in neighbours:
        ok = exists(dr, dc)

        @pl.when(ok)
        def _():
            pl.semaphore_signal(
                barrier, inc=1, device_id={"rows": r + dr, "cols": col + dc}, device_id_type=MESH
            )

        expected = expected + ok.astype(jnp.int32)
    x_peers = [lax.rem(x + d, X) for d in range(1, X)]
    for xp in x_peers:
        pl.semaphore_signal(
            barrier, inc=1, device_id={"rows": r, "cols": xp * cores + c}, device_id_type=MESH
        )

    conv_copies = [
        pltpu.make_async_copy(conv_hbm.at[k], conv_w.at[k], conv_sem.at[k]) for k in range(9)
    ]
    proj_copies = [
        pltpu.make_async_copy(source, proj_w.at[k], proj_sem.at[k])
        for k, source in enumerate((query_hbm, key_hbm, value_hbm, out_hbm))
    ]
    for copy in conv_copies + proj_copies:
        copy.start()

    current = normalize(hidden_ref[...].astype(f32), gain_one_ref[...])
    activated = (current / (1.0 + jnp.exp(-current))).astype(bf16)
    position = lax.broadcasted_iota(jnp.int32, (16, 1), 0)
    for f in range(3):
        frame = activated if f == 2 else cache_ref[f]
        sr[0, f * TC : (f + 1) * TC] = frame[:TC]
        sr[1, f * TC : (f + 1) * TC] = frame[N - TC :]
        wide = frame.astype(f32)
        for i in range(TR):
            k = f * TR + i
            edge[0, k : k + 1] = wide[i * TC : i * TC + 1]
            edge[1, k : k + 1] = wide[(i + 1) * TC - 1 : (i + 1) * TC]
        xs[f, TC : TC + N, C : 2 * C] = frame
        xs[f, TC : TC + N, 0:C] = pltpu.roll(wide, 1, 0).astype(bf16)
        xs[f, TC : TC + N, 2 * C : 3 * C] = pltpu.roll(wide, N - 1, 0).astype(bf16)
    if E > 3 * TR:
        for side in range(2):
            edge[side, 3 * TR : E] = jnp.zeros((E - 3 * TR, C), f32)
    sc[...] = edge[...].astype(bf16)

    pl.semaphore_wait(barrier, expected)

    def halo(dr, dc):
        if dc == 0:
            slot = 1 if dr < 0 else 0
            source, target = sr.at[0 if dr < 0 else 1], hr.at[slot]
        else:
            side = 1 if dc < 0 else 0
            v = 1 - dr
            slot = 2 + side * 3 + v
            source, target = sc.at[0 if dc < 0 else 1], hc.at[side, v]
        return pltpu.make_async_remote_copy(
            src_ref=source, dst_ref=target, send_sem=hsend.at[slot], recv_sem=hrecv.at[slot],
            device_id={"rows": r + dr, "cols": col + dc}, device_id_type=MESH,
        )

    for dr, dc in neighbours:

        @pl.when(exists(dr, dc))
        def _():
            halo(dr, dc).start()

    for dr, dc in neighbours:
        ok = exists(dr, dc)

        @pl.when(ok)
        def _():
            halo(-dr, -dc).wait_recv()

        @pl.when(jnp.logical_not(ok))
        def _():
            if dc == 0:
                hr[0 if dr < 0 else 1] = jnp.zeros((3 * TC, C), bf16)
            else:
                hc[0 if dc < 0 else 1, dr + 1] = jnp.zeros((E, C), bf16)

    sides = [[hc[side, v].astype(f32) for v in range(3)] for side in range(2)]
    for f in range(3):
        for slot, start in ((0, 0), (1, TC + N)):
            line = hr[slot, f * TC : (f + 1) * TC]
            wide = line.astype(f32)
            xs[f, start : start + TC, C : 2 * C] = line
            xs[f, start : start + TC, 0:C] = pltpu.roll(wide, 1, 0).astype(bf16)
            xs[f, start : start + TC, 2 * C : 3 * C] = pltpu.roll(wide, TC - 1, 0).astype(bf16)
        for i in range(TR + 2):
            if i == 0:
                v, k = 0, f * TR + TR - 1
            elif i == TR + 1:
                v, k = 2, f * TR
            else:
                v, k = 1, f * TR + i - 1
            first = slice(i * TC, i * TC + 16)
            last = slice((i + 1) * TC - 16, (i + 1) * TC)
            xs[f, first, 0:C] = jnp.where(
                position == 0, sides[0][v][k : k + 1], xs[f, first, 0:C].astype(f32)
            ).astype(bf16)
            xs[f, last, 2 * C : 3 * C] = jnp.where(
                position == 15, sides[1][v][k : k + 1], xs[f, last, 2 * C : 3 * C].astype(f32)
            ).astype(bf16)

    total = jnp.zeros((N, C), f32)
    for f in range(3):
        for a in range(3):
            conv_copies[f * 3 + a].wait()
            total = total + jnp.dot(
                xs[f, a * TC : a * TC + N], conv_w[f * 3 + a], preferred_element_type=f32
            )
    mixed = (shortcut_ref[...].astype(f32) + (total + conv_bias_ref[...])).astype(bf16)
    o_ref[...] = mixed
    normed = normalize(mixed.astype(f32), gain_two_ref[...]).astype(bf16)

    def span(which):
        return pl.ds(pl.multiple_of(which * N, N), N)

    G[r, span(col)] = normed

    def move(origin, which, send, row_to, col_to):
        block = G.at[origin, span(which)]
        return pltpu.make_async_remote_copy(
            src_ref=block, dst_ref=block, send_sem=send, recv_sem=rsem.at[origin, which],
            device_id={"rows": row_to, "cols": col_to}, device_id_type=MESH,
        )

    def z_move(origin, way):
        return move(origin, col, zsem.at[origin, way], r + (1 if way else -1), col)

    def x_move(origin, d):
        return move(origin, col, xsem.at[origin, d], r, x_peers[d] * cores + c)

    def core_move(origin, xp):
        return move(origin, xp * cores + c, csem.at[origin, xp], r, x * cores + 1 - c)

    def z_conditions(origin):
        return (
            jnp.logical_and(origin >= r, has_up),
            jnp.logical_and(origin <= r, has_down),
        )

    def spread(origin):
        for way, ok in enumerate(z_conditions(origin)):

            @pl.when(ok)
            def _():
                z_move(origin, way).start()

        for d in range(X - 1):
            x_move(origin, d).start()
        if cores == 2:
            core_move(origin, x).start()

    def arrived(origin, which):
        move(origin, which, zsem.at[origin, 0], r, col).wait_recv()

    def relay(origin):
        for xp in x_peers:
            arrived(origin, xp * cores + c)
            if cores == 2:
                core_move(origin, xp).start()

    def at_distance(s, action):
        @pl.when(r - s >= 0)
        def _():
            action(r - s)

        @pl.when(jnp.logical_and(s > 0, r + s < R))
        def _():
            action(r + s)

    spread(r)

    for copy in proj_copies:
        copy.wait()
    queries = (
        jnp.dot(normed, proj_w[0], preferred_element_type=f32) + query_bias_ref[...]
    ).astype(bf16)
    score_scale = float(C) ** (-0.5) * math.log2(math.e)
    contract_last = (((1,), (1,)), ((), ()))
    folded = (
        lax.dot_general(queries, proj_w[1], contract_last, preferred_element_type=f32)
        * score_scale
    ).astype(bf16)
    run_max[...] = jnp.full((N, 1), -1e30, f32)
    run_sum[...] = jnp.zeros((N, 1), f32)
    acc[...] = jnp.zeros((N, C), f32)

    def attend(origin):
        if cores == 2:
            for xp in range(X):
                arrived(origin, xp * cores + 1 - c)
        piece = G[origin]
        scores = lax.dot_general(folded, piece, contract_last, preferred_element_type=f32)
        old_max = run_max[...]
        new_max = jnp.maximum(old_max, jnp.max(scores, axis=1, keepdims=True))
        keep = jnp.exp2(old_max - new_max)
        expos = jnp.exp2(scores - new_max)
        run_max[...] = new_max
        run_sum[...] = run_sum[...] * keep + jnp.sum(expos, axis=1, keepdims=True)
        acc[...] = acc[...] * keep + jnp.dot(
            expos.astype(bf16), piece, preferred_element_type=f32
        )

    def step(s, carry):
        def receive(origin):
            arrived(origin, col)
            spread(origin)

        at_distance(s, receive)
        at_distance(s - 1, relay)
        return carry

    lax.fori_loop(1, R, step, 0)
    at_distance(R - 1, relay)

    def attend_step(s, carry):
        at_distance(s, attend)
        return carry

    lax.fori_loop(0, R, attend_step, 0)

    context = (acc[...] / run_sum[...]).astype(bf16)
    attended = (
        jnp.dot(context, proj_w[2], preferred_element_type=f32) + value_bias_ref[...]
    ).astype(bf16)
    projected = jnp.dot(attended, proj_w[3], preferred_element_type=f32) + out_bias_ref[...]
    o_ref[...] = (o_ref[...].astype(f32) + projected).astype(bf16)

    for dr, dc in neighbours:

        @pl.when(exists(dr, dc))
        def _():
            halo(dr, dc).wait_send()

    def drain(origin, carry):
        for way, ok in enumerate(z_conditions(origin)):

            @pl.when(ok)
            def _():
                z_move(origin, way).wait_send()

        for d in range(X - 1):
            x_move(origin, d).wait_send()
        if cores == 2:
            for xp in range(X):
                core_move(origin, xp).wait_send()
        return carry

    lax.fori_loop(0, R, drain, 0)


def per_device(
    hidden,
    frame_cache,
    shortcut,
    gain_one,
    conv_weight,
    conv_bias,
    gain_two,
    query_weight,
    query_bias,
    key_weight,
    value_weight,
    value_bias,
    out_weight,
    out_bias,
):
    _, TR, TC, C = hidden.shape
    N = TR * TC
    R = lax.axis_size("rows")
    K = lax.axis_size("cols")
    cores = 2 if K % 2 == 0 else 1
    X = K // cores
    E = -(-3 * TR // 16) * 16
    vector = lambda v: v.reshape(1, C)
    vmem = pl.BlockSpec(memory_space=pltpu.VMEM)
    hbm = pl.BlockSpec(memory_space=pltpu.HBM)
    dma = pltpu.SemaphoreType.DMA
    flops = 2 * N * C * (27 * C + 5 * C + 2 * R * K * N)
    decoded = pl.pallas_call(
        functools.partial(kernel, R, K, cores, TR, TC, C, E),
        out_shape=jax.ShapeDtypeStruct((N, C), bf16),
        in_specs=[vmem] * 9 + [hbm] * 5,
        out_specs=vmem,
        scratch_shapes=[
            pltpu.VMEM((9, 3 * C, C), bf16),
            pltpu.VMEM((4, C, C), bf16),
            pltpu.VMEM((3, N + 2 * TC, 3 * C), bf16),
            pltpu.VMEM((2, 3 * TC, C), bf16),
            pltpu.VMEM((2, E, C), bf16),
            pltpu.VMEM((2, 3 * TC, C), bf16),
            pltpu.VMEM((2, 3, E, C), bf16),
            pltpu.VMEM((2, E, C), f32),
            pltpu.VMEM((R, K * N, C), bf16),
            pltpu.VMEM((N, 1), f32),
            pltpu.VMEM((N, 1), f32),
            pltpu.VMEM((N, C), f32),
            dma((9,)),
            dma((4,)),
            dma((8,)),
            dma((8,)),
            dma((R, 2)),
            dma((R, max(X - 1, 1))),
            dma((R, X)),
            dma((R, K)),
        ],
        compiler_params=pltpu.CompilerParams(
            collective_id=0, has_side_effects=True, vmem_limit_bytes=48 * 1024 * 1024
        ),
        cost_estimate=pl.CostEstimate(
            flops=flops, bytes_accessed=2 * C * (32 * C + 6 * N), transcendentals=R * K * N * N
        ),
    )(
        hidden.reshape(N, C),
        frame_cache.reshape(2, N, C),
        shortcut.reshape(N, C),
        vector(gain_one),
        vector(conv_bias),
        vector(gain_two),
        vector(query_bias),
        vector(value_bias),
        vector(out_bias),
        conv_weight.reshape(9, 3 * C, C),
        query_weight,
        key_weight,
        value_weight,
        out_weight,
    )
    return decoded.reshape(1, TR, TC, C)


def solution(mesh):
    placed = (
        P("videos", "rows", "cols", None),
        P("videos", None, "rows", "cols", None),
        P("videos", "rows", "cols", None),
        P(),
        P(),
        P(),
        P(),
        P(),
        P(),
        P(),
        P(),
        P(),
        P(),
        P(),
    )
    return jax.shard_map(
        per_device,
        mesh=mesh,
        in_specs=placed,
        out_specs=P("videos", "rows", "cols", None),
        check_vma=False,
    )
```

```python
import functools
import math

import jax
import jax.numpy as jnp
from jax import lax
from jax.experimental import pallas as pl
from jax.experimental.pallas import tpu as pltpu
from jax.sharding import PartitionSpec as P

norm_epsilon = 1e-06
f32 = jnp.float32
bf16 = jnp.bfloat16
MESH = pl.DeviceIdType.MESH


def normalize(field_rows, gain):
    mean_square = jnp.mean(field_rows * field_rows, axis=1, keepdims=True)
    return field_rows * lax.rsqrt(mean_square + norm_epsilon) * gain


def kernel(
    R, K, cores, TR, TC, C, E,
    hidden_hbm, cache_hbm, shortcut_hbm, gain_one_hbm, conv_bias_hbm, gain_two_hbm,
    query_bias_hbm, value_bias_hbm, out_bias_hbm,
    conv_hbm, query_hbm, key_hbm, value_hbm, out_hbm,
    o_ref,
    hidden_ref, cache_ref, shortcut_ref, gain_one_ref, conv_bias_ref, gain_two_ref,
    query_bias_ref, value_bias_ref, out_bias_ref,
    conv_w, proj_w, xs, sr, sc, hr, hc, edge, G, run_max, run_sum, acc,
    in_sem, conv_sem, proj_sem, hsend, hrecv, zsem, xsem, csem, rsem,
):
    X = K // cores
    N = TR * TC
    r = lax.axis_index("rows")
    col = lax.axis_index("cols")
    x = col // cores
    c = col % cores

    in_copies = [
        pltpu.make_async_copy(source, target, in_sem.at[k])
        for k, (source, target) in enumerate(
            (
                (hidden_hbm, hidden_ref),
                (gain_one_hbm, gain_one_ref),
                (cache_hbm, cache_ref),
                (shortcut_hbm, shortcut_ref),
                (conv_bias_hbm, conv_bias_ref),
                (gain_two_hbm, gain_two_ref),
                (query_bias_hbm, query_bias_ref),
                (value_bias_hbm, value_bias_ref),
                (out_bias_hbm, out_bias_ref),
            )
        )
    ]
    for copy in in_copies:
        copy.start()

    has_up = r > 0
    has_down = r < R - 1
    rows_ok = (has_up, None, has_down)

    def exists(dr, dc):
        ok = None
        if dr:
            ok = rows_ok[dr + 1]
        if dc:
            side = (col > 0) if dc < 0 else (col < K - 1)
            ok = side if ok is None else jnp.logical_and(ok, side)
        return ok

    neighbours = [(-1, 0), (1, 0)] + [(dr, dc) for dc in (-1, 1) for dr in (-1, 0, 1)]
    barrier = pltpu.get_barrier_semaphore()
    expected = jnp.int32(X - 1)
    for dr, dc in neighbours:
        ok = exists(dr, dc)

        @pl.when(ok)
        def _():
            pl.semaphore_signal(
                barrier, inc=1, device_id={"rows": r + dr, "cols": col + dc}, device_id_type=MESH
            )

        expected = expected + ok.astype(jnp.int32)
    x_peers = [lax.rem(x + d, X) for d in range(1, X)]
    for xp in x_peers:
        pl.semaphore_signal(
            barrier, inc=1, device_id={"rows": r, "cols": xp * cores + c}, device_id_type=MESH
        )

    conv_copies = [
        pltpu.make_async_copy(conv_hbm.at[k], conv_w.at[k], conv_sem.at[k]) for k in range(9)
    ]
    proj_copies = [
        pltpu.make_async_copy(source, proj_w.at[k], proj_sem.at[k])
        for k, source in enumerate((query_hbm, key_hbm, value_hbm, out_hbm))
    ]
    for copy in conv_copies + proj_copies:
        copy.start()

    for copy in in_copies[:3]:
        copy.wait()
    current = normalize(hidden_ref[...].astype(f32), gain_one_ref[...])
    activated = (current / (1.0 + jnp.exp(-current))).astype(bf16)
    position = lax.broadcasted_iota(jnp.int32, (16, 1), 0)
    for f in range(3):
        frame = activated if f == 2 else cache_ref[f]
        sr[0, f * TC : (f + 1) * TC] = frame[:TC]
        sr[1, f * TC : (f + 1) * TC] = frame[N - TC :]
        wide = frame.astype(f32)
        for i in range(TR):
            k = f * TR + i
            edge[0, k : k + 1] = wide[i * TC : i * TC + 1]
            edge[1, k : k + 1] = wide[(i + 1) * TC - 1 : (i + 1) * TC]
        xs[f, TC : TC + N, C : 2 * C] = frame
        xs[f, TC : TC + N, 0:C] = pltpu.roll(wide, 1, 0).astype(bf16)
        xs[f, TC : TC + N, 2 * C : 3 * C] = pltpu.roll(wide, N - 1, 0).astype(bf16)
    if E > 3 * TR:
        for side in range(2):
            edge[side, 3 * TR : E] = jnp.zeros((E - 3 * TR, C), f32)
    sc[...] = edge[...].astype(bf16)

    pl.semaphore_wait(barrier, expected)

    def halo(dr, dc):
        if dc == 0:
            slot = 1 if dr < 0 else 0
            source, target = sr.at[0 if dr < 0 else 1], hr.at[slot]
        else:
            side = 1 if dc < 0 else 0
            v = 1 - dr
            slot = 2 + side * 3 + v
            source, target = sc.at[0 if dc < 0 else 1], hc.at[side, v]
        return pltpu.make_async_remote_copy(
            src_ref=source, dst_ref=target, send_sem=hsend.at[slot], recv_sem=hrecv.at[slot],
            device_id={"rows": r + dr, "cols": col + dc}, device_id_type=MESH,
        )

    for dr, dc in neighbours:

        @pl.when(exists(dr, dc))
        def _():
            halo(dr, dc).start()

    for dr, dc in neighbours:
        ok = exists(dr, dc)

        @pl.when(ok)
        def _():
            halo(-dr, -dc).wait_recv()

        @pl.when(jnp.logical_not(ok))
        def _():
            if dc == 0:
                hr[0 if dr < 0 else 1] = jnp.zeros((3 * TC, C), bf16)
            else:
                hc[0 if dc < 0 else 1, dr + 1] = jnp.zeros((E, C), bf16)

    sides = [[hc[side, v].astype(f32) for v in range(3)] for side in range(2)]
    for f in range(3):
        for slot, start in ((0, 0), (1, TC + N)):
            line = hr[slot, f * TC : (f + 1) * TC]
            wide = line.astype(f32)
            xs[f, start : start + TC, C : 2 * C] = line
            xs[f, start : start + TC, 0:C] = pltpu.roll(wide, 1, 0).astype(bf16)
            xs[f, start : start + TC, 2 * C : 3 * C] = pltpu.roll(wide, TC - 1, 0).astype(bf16)
        for i in range(TR + 2):
            if i == 0:
                v, k = 0, f * TR + TR - 1
            elif i == TR + 1:
                v, k = 2, f * TR
            else:
                v, k = 1, f * TR + i - 1
            first = slice(i * TC, i * TC + 16)
            last = slice((i + 1) * TC - 16, (i + 1) * TC)
            xs[f, first, 0:C] = jnp.where(
                position == 0, sides[0][v][k : k + 1], xs[f, first, 0:C].astype(f32)
            ).astype(bf16)
            xs[f, last, 2 * C : 3 * C] = jnp.where(
                position == 15, sides[1][v][k : k + 1], xs[f, last, 2 * C : 3 * C].astype(f32)
            ).astype(bf16)

    for copy in in_copies[3:]:
        copy.wait()
    total = jnp.zeros((N, C), f32)
    for f in range(3):
        for a in range(3):
            conv_copies[f * 3 + a].wait()
            total = total + jnp.dot(
                xs[f, a * TC : a * TC + N], conv_w[f * 3 + a], preferred_element_type=f32
            )
    mixed = (shortcut_ref[...].astype(f32) + (total + conv_bias_ref[...])).astype(bf16)
    o_ref[...] = mixed
    normed = normalize(mixed.astype(f32), gain_two_ref[...]).astype(bf16)

    def span(which):
        return pl.ds(pl.multiple_of(which * N, N), N)

    G[r, span(col)] = normed

    def move(origin, which, send, row_to, col_to):
        block = G.at[origin, span(which)]
        return pltpu.make_async_remote_copy(
            src_ref=block, dst_ref=block, send_sem=send, recv_sem=rsem.at[origin, which],
            device_id={"rows": row_to, "cols": col_to}, device_id_type=MESH,
        )

    def z_move(origin, way):
        return move(origin, col, zsem.at[origin, way], r + (1 if way else -1), col)

    def x_move(origin, d):
        return move(origin, col, xsem.at[origin, d], r, x_peers[d] * cores + c)

    def core_move(origin, xp):
        return move(origin, xp * cores + c, csem.at[origin, xp], r, x * cores + 1 - c)

    def z_conditions(origin):
        return (
            jnp.logical_and(origin >= r, has_up),
            jnp.logical_and(origin <= r, has_down),
        )

    def spread(origin):
        for way, ok in enumerate(z_conditions(origin)):

            @pl.when(ok)
            def _():
                z_move(origin, way).start()

        for d in range(X - 1):
            x_move(origin, d).start()
        if cores == 2:
            core_move(origin, x).start()

    def arrived(origin, which):
        move(origin, which, zsem.at[origin, 0], r, col).wait_recv()

    def relay(origin):
        for xp in x_peers:
            arrived(origin, xp * cores + c)
            if cores == 2:
                core_move(origin, xp).start()

    def at_distance(s, action):
        @pl.when(jnp.logical_and(s >= 0, r - s >= 0))
        def _():
            action(r - s)

        @pl.when(jnp.logical_and(s > 0, r + s < R))
        def _():
            action(r + s)

    spread(r)

    for copy in proj_copies:
        copy.wait()
    queries = (
        jnp.dot(normed, proj_w[0], preferred_element_type=f32) + query_bias_ref[...]
    ).astype(bf16)
    score_scale = float(C) ** (-0.5) * math.log2(math.e)
    contract_last = (((1,), (1,)), ((), ()))
    folded = (
        lax.dot_general(queries, proj_w[1], contract_last, preferred_element_type=f32)
        * score_scale
    ).astype(bf16)
    run_max[...] = jnp.full((N, 1), -1e30, f32)
    run_sum[...] = jnp.zeros((N, 1), f32)
    acc[...] = jnp.zeros((N, C), f32)

    def attend(origin):
        if cores == 2:
            for xp in range(X):
                arrived(origin, xp * cores + 1 - c)
        piece = G[origin]
        scores = lax.dot_general(folded, piece, contract_last, preferred_element_type=f32)
        old_max = run_max[...]
        new_max = jnp.maximum(old_max, jnp.max(scores, axis=1, keepdims=True))
        keep = jnp.exp2(old_max - new_max)
        expos = jnp.exp2(scores - new_max)
        run_max[...] = new_max
        run_sum[...] = run_sum[...] * keep + jnp.sum(expos, axis=1, keepdims=True)
        acc[...] = acc[...] * keep + jnp.dot(
            expos.astype(bf16), piece, preferred_element_type=f32
        )

    def step(s, carry):
        def receive(origin):
            arrived(origin, col)
            spread(origin)

        at_distance(s, receive)
        at_distance(s - 1, relay)
        at_distance(s - 2, attend)
        return carry

    lax.fori_loop(1, R, step, 0)
    at_distance(R - 1, relay)

    def attend_step(s, carry):
        at_distance(s, attend)
        return carry

    lax.fori_loop(max(R - 2, 0), R, attend_step, 0)

    context = (acc[...] / run_sum[...]).astype(bf16)
    attended = (
        jnp.dot(context, proj_w[2], preferred_element_type=f32) + value_bias_ref[...]
    ).astype(bf16)
    projected = jnp.dot(attended, proj_w[3], preferred_element_type=f32) + out_bias_ref[...]
    o_ref[...] = (o_ref[...].astype(f32) + projected).astype(bf16)

    for dr, dc in neighbours:

        @pl.when(exists(dr, dc))
        def _():
            halo(dr, dc).wait_send()

    def drain(origin, carry):
        for way, ok in enumerate(z_conditions(origin)):

            @pl.when(ok)
            def _():
                z_move(origin, way).wait_send()

        for d in range(X - 1):
            x_move(origin, d).wait_send()
        if cores == 2:
            for xp in range(X):
                core_move(origin, xp).wait_send()
        return carry

    lax.fori_loop(0, R, drain, 0)


def per_device(
    hidden,
    frame_cache,
    shortcut,
    gain_one,
    conv_weight,
    conv_bias,
    gain_two,
    query_weight,
    query_bias,
    key_weight,
    value_weight,
    value_bias,
    out_weight,
    out_bias,
):
    _, TR, TC, C = hidden.shape
    N = TR * TC
    R = lax.axis_size("rows")
    K = lax.axis_size("cols")
    cores = 2 if K % 2 == 0 else 1
    X = K // cores
    E = -(-3 * TR // 16) * 16
    vmem = pl.BlockSpec(memory_space=pltpu.VMEM)
    hbm = pl.BlockSpec(memory_space=pltpu.HBM)
    dma = pltpu.SemaphoreType.DMA
    flops = 2 * N * C * (27 * C + 5 * C + 2 * R * K * N)
    decoded = pl.pallas_call(
        functools.partial(kernel, R, K, cores, TR, TC, C, E),
        out_shape=jax.ShapeDtypeStruct((N, C), bf16),
        in_specs=[hbm] * 14,
        out_specs=vmem,
        scratch_shapes=[
            pltpu.VMEM((N, C), bf16),
            pltpu.VMEM((2, N, C), bf16),
            pltpu.VMEM((N, C), bf16),
        ]
        + [pltpu.VMEM((C,), f32)] * 6
        + [
            pltpu.VMEM((9, 3 * C, C), bf16),
            pltpu.VMEM((4, C, C), bf16),
            pltpu.VMEM((3, N + 2 * TC, 3 * C), bf16),
            pltpu.VMEM((2, 3 * TC, C), bf16),
            pltpu.VMEM((2, E, C), bf16),
            pltpu.VMEM((2, 3 * TC, C), bf16),
            pltpu.VMEM((2, 3, E, C), bf16),
            pltpu.VMEM((2, E, C), f32),
            pltpu.VMEM((R, K * N, C), bf16),
            pltpu.VMEM((N, 1), f32),
            pltpu.VMEM((N, 1), f32),
            pltpu.VMEM((N, C), f32),
            dma((9,)),
            dma((9,)),
            dma((4,)),
            dma((8,)),
            dma((8,)),
            dma((R, 2)),
            dma((R, max(X - 1, 1))),
            dma((R, X)),
            dma((R, K)),
        ],
        compiler_params=pltpu.CompilerParams(
            collective_id=0, has_side_effects=True, vmem_limit_bytes=63 * 1024 * 1024
        ),
        cost_estimate=pl.CostEstimate(
            flops=flops, bytes_accessed=2 * C * (32 * C + 6 * N), transcendentals=R * K * N * N
        ),
    )(
        hidden.reshape(N, C),
        frame_cache.reshape(2, N, C),
        shortcut.reshape(N, C),
        gain_one,
        conv_bias,
        gain_two,
        query_bias,
        value_bias,
        out_bias,
        conv_weight.reshape(9, 3 * C, C),
        query_weight,
        key_weight,
        value_weight,
        out_weight,
    )
    return decoded.reshape(1, TR, TC, C)


def solution(mesh):
    placed = (
        P("videos", "rows", "cols", None),
        P("videos", None, "rows", "cols", None),
        P("videos", "rows", "cols", None),
        P(),
        P(),
        P(),
        P(),
        P(),
        P(),
        P(),
        P(),
        P(),
        P(),
        P(),
    )
    return jax.shard_map(
        per_device,
        mesh=mesh,
        in_specs=placed,
        out_specs=P("videos", "rows", "cols", None),
        check_vma=False,
    )
```

```python
import functools
import math

import jax
import jax.numpy as jnp
from jax import lax
from jax.experimental import pallas as pl
from jax.experimental.pallas import tpu as pltpu
from jax.sharding import PartitionSpec as P

norm_epsilon = 1e-06
pieces = 2
f32 = jnp.float32
bf16 = jnp.bfloat16
MESH = pl.DeviceIdType.MESH


def normalize(field_rows, gain):
    mean_square = jnp.mean(field_rows * field_rows, axis=1, keepdims=True)
    return field_rows * lax.rsqrt(mean_square + norm_epsilon) * gain


def kernel(
    R, K, cores, TR, TC, C, E,
    hidden_hbm, cache_hbm, shortcut_hbm, gain_one_hbm, conv_bias_hbm, gain_two_hbm,
    query_bias_hbm, value_bias_hbm, out_bias_hbm,
    conv_hbm, query_hbm, key_hbm, value_hbm, out_hbm,
    o_ref,
    hidden_ref, cache_ref, shortcut_ref, gain_one_ref, conv_bias_ref, gain_two_ref,
    query_bias_ref, value_bias_ref, out_bias_ref,
    conv_w, proj_w, xs, sr, sc, hr, hc, edge, G, run_max, run_sum, acc,
    in_sem, conv_sem, proj_sem, hsend, hrecv, zsem, xsem, csem, rsem,
):
    X = K // cores
    N = TR * TC
    M = N // pieces
    r = lax.axis_index("rows")
    col = lax.axis_index("cols")
    x = col // cores
    c = col % cores

    in_copies = [
        pltpu.make_async_copy(source, target, in_sem.at[k])
        for k, (source, target) in enumerate(
            (
                (hidden_hbm, hidden_ref),
                (gain_one_hbm, gain_one_ref),
                (cache_hbm, cache_ref),
                (shortcut_hbm, shortcut_ref),
                (conv_bias_hbm, conv_bias_ref),
                (gain_two_hbm, gain_two_ref),
                (query_bias_hbm, query_bias_ref),
                (value_bias_hbm, value_bias_ref),
                (out_bias_hbm, out_bias_ref),
            )
        )
    ]
    for copy in in_copies:
        copy.start()

    has_up = r > 0
    has_down = r < R - 1
    rows_ok = (has_up, None, has_down)

    def exists(dr, dc):
        ok = None
        if dr:
            ok = rows_ok[dr + 1]
        if dc:
            side = (col > 0) if dc < 0 else (col < K - 1)
            ok = side if ok is None else jnp.logical_and(ok, side)
        return ok

    neighbours = [(-1, 0), (1, 0)] + [(dr, dc) for dc in (-1, 1) for dr in (-1, 0, 1)]
    barrier = pltpu.get_barrier_semaphore()
    expected = jnp.int32(X - 1)
    for dr, dc in neighbours:
        ok = exists(dr, dc)

        @pl.when(ok)
        def _():
            pl.semaphore_signal(
                barrier, inc=1, device_id={"rows": r + dr, "cols": col + dc}, device_id_type=MESH
            )

        expected = expected + ok.astype(jnp.int32)
    x_peers = [lax.rem(x + d, X) for d in range(1, X)]
    for xp in x_peers:
        pl.semaphore_signal(
            barrier, inc=1, device_id={"rows": r, "cols": xp * cores + c}, device_id_type=MESH
        )

    conv_copies = [
        pltpu.make_async_copy(conv_hbm.at[k], conv_w.at[k], conv_sem.at[k]) for k in range(9)
    ]
    proj_copies = [
        pltpu.make_async_copy(source, proj_w.at[k], proj_sem.at[k])
        for k, source in enumerate((query_hbm, key_hbm, value_hbm, out_hbm))
    ]
    for copy in conv_copies + proj_copies:
        copy.start()

    for copy in in_copies[:3]:
        copy.wait()
    current = normalize(hidden_ref[...].astype(f32), gain_one_ref[...])
    activated = (current / (1.0 + jnp.exp(-current))).astype(bf16)
    position = lax.broadcasted_iota(jnp.int32, (16, 1), 0)
    for f in range(3):
        frame = activated if f == 2 else cache_ref[f]
        sr[0, f * TC : (f + 1) * TC] = frame[:TC]
        sr[1, f * TC : (f + 1) * TC] = frame[N - TC :]
        wide = frame.astype(f32)
        for i in range(TR):
            k = f * TR + i
            edge[0, k : k + 1] = wide[i * TC : i * TC + 1]
            edge[1, k : k + 1] = wide[(i + 1) * TC - 1 : (i + 1) * TC]
    if E > 3 * TR:
        for side in range(2):
            edge[side, 3 * TR : E] = jnp.zeros((E - 3 * TR, C), f32)
    sc[...] = edge[...].astype(bf16)

    pl.semaphore_wait(barrier, expected)

    def halo(dr, dc):
        if dc == 0:
            slot = 1 if dr < 0 else 0
            source, target = sr.at[0 if dr < 0 else 1], hr.at[slot]
        else:
            side = 1 if dc < 0 else 0
            v = 1 - dr
            slot = 2 + side * 3 + v
            source, target = sc.at[0 if dc < 0 else 1], hc.at[side, v]
        return pltpu.make_async_remote_copy(
            src_ref=source, dst_ref=target, send_sem=hsend.at[slot], recv_sem=hrecv.at[slot],
            device_id={"rows": r + dr, "cols": col + dc}, device_id_type=MESH,
        )

    for dr, dc in neighbours:

        @pl.when(exists(dr, dc))
        def _():
            halo(dr, dc).start()

    for f in range(3):
        frame = activated if f == 2 else cache_ref[f]
        wide = frame.astype(f32)
        xs[f, TC : TC + N, C : 2 * C] = frame
        xs[f, TC : TC + N, 0:C] = pltpu.roll(wide, 1, 0).astype(bf16)
        xs[f, TC : TC + N, 2 * C : 3 * C] = pltpu.roll(wide, N - 1, 0).astype(bf16)

    for dr, dc in neighbours:
        ok = exists(dr, dc)

        @pl.when(ok)
        def _():
            halo(-dr, -dc).wait_recv()

        @pl.when(jnp.logical_not(ok))
        def _():
            if dc == 0:
                hr[0 if dr < 0 else 1] = jnp.zeros((3 * TC, C), bf16)
            else:
                hc[0 if dc < 0 else 1, dr + 1] = jnp.zeros((E, C), bf16)

    sides = [[hc[side, v].astype(f32) for v in range(3)] for side in range(2)]
    for f in range(3):
        for slot, start in ((0, 0), (1, TC + N)):
            line = hr[slot, f * TC : (f + 1) * TC]
            wide = line.astype(f32)
            xs[f, start : start + TC, C : 2 * C] = line
            xs[f, start : start + TC, 0:C] = pltpu.roll(wide, 1, 0).astype(bf16)
            xs[f, start : start + TC, 2 * C : 3 * C] = pltpu.roll(wide, TC - 1, 0).astype(bf16)
        for i in range(TR + 2):
            if i == 0:
                v, k = 0, f * TR + TR - 1
            elif i == TR + 1:
                v, k = 2, f * TR
            else:
                v, k = 1, f * TR + i - 1
            first = slice(i * TC, i * TC + 16)
            last = slice((i + 1) * TC - 16, (i + 1) * TC)
            xs[f, first, 0:C] = jnp.where(
                position == 0, sides[0][v][k : k + 1], xs[f, first, 0:C].astype(f32)
            ).astype(bf16)
            xs[f, last, 2 * C : 3 * C] = jnp.where(
                position == 15, sides[1][v][k : k + 1], xs[f, last, 2 * C : 3 * C].astype(f32)
            ).astype(bf16)

    for copy in in_copies[3:]:
        copy.wait()
    total = jnp.zeros((N, C), f32)
    for f in range(3):
        for a in range(3):
            conv_copies[f * 3 + a].wait()
            total = total + jnp.dot(
                xs[f, a * TC : a * TC + N], conv_w[f * 3 + a], preferred_element_type=f32
            )
    mixed = (shortcut_ref[...].astype(f32) + (total + conv_bias_ref[...])).astype(bf16)
    o_ref[...] = mixed
    normed = normalize(mixed.astype(f32), gain_two_ref[...]).astype(bf16)

    def span(which):
        return pl.ds(pl.multiple_of(which * N, N), N)

    G[r, span(col)] = normed

    def move(origin, which, piece, send, row_to, col_to):
        start = pl.multiple_of(which * N + piece * M, M)
        block = G.at[origin, pl.ds(start, M)]
        return pltpu.make_async_remote_copy(
            src_ref=block, dst_ref=block, send_sem=send, recv_sem=rsem.at[origin, which, piece],
            device_id={"rows": row_to, "cols": col_to}, device_id_type=MESH,
        )

    def z_move(origin, way, h):
        return move(origin, col, h, zsem.at[origin, way, h], r + (1 if way else -1), col)

    def x_move(origin, d, h):
        return move(origin, col, h, xsem.at[origin, d, h], r, x_peers[d] * cores + c)

    def core_move(origin, xp, h):
        return move(origin, xp * cores + c, h, csem.at[origin, xp, h], r, x * cores + 1 - c)

    def z_conditions(origin):
        return (
            jnp.logical_and(origin >= r, has_up),
            jnp.logical_and(origin <= r, has_down),
        )

    def spread(origin, h):
        for way, ok in enumerate(z_conditions(origin)):

            @pl.when(ok)
            def _():
                z_move(origin, way, h).start()

        for d in range(X - 1):
            x_move(origin, d, h).start()
        if cores == 2:
            core_move(origin, x, h).start()

    def arrived(origin, which, h):
        move(origin, which, h, zsem.at[origin, 0, h], r, col).wait_recv()

    def relay(origin):
        for h in range(pieces):
            for xp in x_peers:
                arrived(origin, xp * cores + c, h)
                if cores == 2:
                    core_move(origin, xp, h).start()

    def at_distance(s, action):
        @pl.when(jnp.logical_and(s >= 0, r - s >= 0))
        def _():
            action(r - s)

        @pl.when(jnp.logical_and(s > 0, r + s < R))
        def _():
            action(r + s)

    for h in range(pieces):
        spread(r, h)

    for copy in proj_copies:
        copy.wait()
    queries = (
        jnp.dot(normed, proj_w[0], preferred_element_type=f32) + query_bias_ref[...]
    ).astype(bf16)
    score_scale = float(C) ** (-0.5) * math.log2(math.e)
    contract_last = (((1,), (1,)), ((), ()))
    folded = (
        lax.dot_general(queries, proj_w[1], contract_last, preferred_element_type=f32)
        * score_scale
    ).astype(bf16)
    run_max[...] = jnp.full((N, 1), -1e30, f32)
    run_sum[...] = jnp.zeros((N, 1), f32)
    acc[...] = jnp.zeros((N, C), f32)

    def attend(origin):
        if cores == 2:
            for xp in range(X):
                for h in range(pieces):
                    arrived(origin, xp * cores + 1 - c, h)
        piece = G[origin]
        scores = lax.dot_general(folded, piece, contract_last, preferred_element_type=f32)
        old_max = run_max[...]
        new_max = jnp.maximum(old_max, jnp.max(scores, axis=1, keepdims=True))
        keep = jnp.exp2(old_max - new_max)
        expos = jnp.exp2(scores - new_max)
        run_max[...] = new_max
        run_sum[...] = run_sum[...] * keep + jnp.sum(expos, axis=1, keepdims=True)
        acc[...] = acc[...] * keep + jnp.dot(
            expos.astype(bf16), piece, preferred_element_type=f32
        )

    def step(s, carry):
        for h in range(pieces):

            def receive(origin):
                arrived(origin, col, h)
                spread(origin, h)

            at_distance(s, receive)
        at_distance(s - 1, relay)
        at_distance(s - 2, attend)
        return carry

    lax.fori_loop(1, R, step, 0)
    at_distance(R - 1, relay)

    def attend_step(s, carry):
        at_distance(s, attend)
        return carry

    lax.fori_loop(max(R - 2, 0), R, attend_step, 0)

    context = (acc[...] / run_sum[...]).astype(bf16)
    attended = (
        jnp.dot(context, proj_w[2], preferred_element_type=f32) + value_bias_ref[...]
    ).astype(bf16)
    projected = jnp.dot(attended, proj_w[3], preferred_element_type=f32) + out_bias_ref[...]
    o_ref[...] = (o_ref[...].astype(f32) + projected).astype(bf16)

    for dr, dc in neighbours:

        @pl.when(exists(dr, dc))
        def _():
            halo(dr, dc).wait_send()

    def drain(origin, carry):
        for h in range(pieces):
            for way, ok in enumerate(z_conditions(origin)):

                @pl.when(ok)
                def _():
                    z_move(origin, way, h).wait_send()

            for d in range(X - 1):
                x_move(origin, d, h).wait_send()
            if cores == 2:
                for xp in range(X):
                    core_move(origin, xp, h).wait_send()
        return carry

    lax.fori_loop(0, R, drain, 0)


def per_device(
    hidden,
    frame_cache,
    shortcut,
    gain_one,
    conv_weight,
    conv_bias,
    gain_two,
    query_weight,
    query_bias,
    key_weight,
    value_weight,
    value_bias,
    out_weight,
    out_bias,
):
    _, TR, TC, C = hidden.shape
    N = TR * TC
    R = lax.axis_size("rows")
    K = lax.axis_size("cols")
    cores = 2 if K % 2 == 0 else 1
    X = K // cores
    E = -(-3 * TR // 16) * 16
    vmem = pl.BlockSpec(memory_space=pltpu.VMEM)
    hbm = pl.BlockSpec(memory_space=pltpu.HBM)
    dma = pltpu.SemaphoreType.DMA
    flops = 2 * N * C * (27 * C + 5 * C + 2 * R * K * N)
    decoded = pl.pallas_call(
        functools.partial(kernel, R, K, cores, TR, TC, C, E),
        out_shape=jax.ShapeDtypeStruct((N, C), bf16),
        in_specs=[hbm] * 14,
        out_specs=vmem,
        scratch_shapes=[
            pltpu.VMEM((N, C), bf16),
            pltpu.VMEM((2, N, C), bf16),
            pltpu.VMEM((N, C), bf16),
        ]
        + [pltpu.VMEM((C,), f32)] * 6
        + [
            pltpu.VMEM((9, 3 * C, C), bf16),
            pltpu.VMEM((4, C, C), bf16),
            pltpu.VMEM((3, N + 2 * TC, 3 * C), bf16),
            pltpu.VMEM((2, 3 * TC, C), bf16),
            pltpu.VMEM((2, E, C), bf16),
            pltpu.VMEM((2, 3 * TC, C), bf16),
            pltpu.VMEM((2, 3, E, C), bf16),
            pltpu.VMEM((2, E, C), f32),
            pltpu.VMEM((R, K * N, C), bf16),
            pltpu.VMEM((N, 1), f32),
            pltpu.VMEM((N, 1), f32),
            pltpu.VMEM((N, C), f32),
            dma((9,)),
            dma((9,)),
            dma((4,)),
            dma((8,)),
            dma((8,)),
            dma((R, 2, pieces)),
            dma((R, max(X - 1, 1), pieces)),
            dma((R, X, pieces)),
            dma((R, K, pieces)),
        ],
        compiler_params=pltpu.CompilerParams(
            collective_id=0, has_side_effects=True, vmem_limit_bytes=48 * 1024 * 1024
        ),
        cost_estimate=pl.CostEstimate(
            flops=flops, bytes_accessed=2 * C * (32 * C + 6 * N), transcendentals=R * K * N * N
        ),
    )
    operands = (
        hidden.reshape(N, C),
        frame_cache.reshape(2, N, C),
        shortcut.reshape(N, C),
        gain_one,
        conv_bias,
        gain_two,
        query_bias,
        value_bias,
        out_bias,
        conv_weight.reshape(9, 3 * C, C),
        query_weight,
        key_weight,
        value_weight,
        out_weight,
    )
    decoded = decoded(*[pltpu.with_memory_space_constraint(v, pltpu.HBM) for v in operands])
    return decoded.reshape(1, TR, TC, C)


def solution(mesh):
    placed = (
        P("videos", "rows", "cols", None),
        P("videos", None, "rows", "cols", None),
        P("videos", "rows", "cols", None),
        P(),
        P(),
        P(),
        P(),
        P(),
        P(),
        P(),
        P(),
        P(),
        P(),
        P(),
    )
    return jax.shard_map(
        per_device,
        mesh=mesh,
        in_specs=placed,
        out_specs=P("videos", "rows", "cols", None),
        check_vma=False,
    )
```
